32 devices in a mesh: pipe: 2 (over x), tensor: 4 (over y, core), dp: 4 (over z).
Axes of the slice: x: 2, y: 2, z: 4, core: 2. Of those that a mesh axis runs over, the one named last changes fastest.
Arguments:
- tokens: bfloat16 [4, 128, 4096], P('dp'), may hold values from -600 to 600
- norm_gains: float32 [2, 4096], P('pipe'), may hold values from 0.5 to 1.5
- qkv_weight: bfloat16 [2, 4096, 6144], P('pipe', 'dp', 'tensor'), may hold values from -0.1875 to 0.1875
- out_weight: bfloat16 [2, 4096, 4096], P('pipe', 'dp', 'tensor'), may hold values from -0.09375 to 0.09375
- cotangent: bfloat16 [4, 128, 4096], P('dp'), may hold values from -2.5 to 2.5
Outputs:
- qkv_grad: float32 [2, 4096, 6144], P('pipe', 'dp', 'tensor')
- out_grad: float32 [2, 4096, 4096], P('pipe', 'dp', 'tensor')
- gain_grad: float32 [2, 4096], P('pipe', 'dp')
The draws below stay inside these ranges and needn't reach their ends.
All inputs are finite; a program needn't handle non-finite values.
Results may differ from the reference program's by a relative error of at most 0.025.
Values may be sent and summed in bfloat16 or wider, within the bound.
A program may use at most 128 MiB of HBM per device.

```python
import jax
import jax.numpy as jnp
from jax import lax

D = 4096
HD = 128
KVH = 8
GROUP = 4
SEQ = 128
LAYERS = 2
SEQS = 4


def draw_tokens(key, part):
    values = jnp.clip(jax.random.normal(jax.random.fold_in(key, 11), (SEQS, SEQ, D), jnp.float32), -6.0, 6.0)
    return values.astype(jnp.bfloat16)


def draw_qkv_weight(key, part):
    columns = KVH * (GROUP + 2) * HD
    values = jnp.clip(jax.random.normal(jax.random.fold_in(key, 21), (LAYERS, D, columns), jnp.float32), -6.0, 6.0) * D ** (-0.5)
    return values.astype(jnp.bfloat16)


def steps_of(key, dims, shards, low, top_value):
    gain, own = 1.0, jax.random.fold_in(key, 6)
    for axis_at, blocks in shards:
        steps = jnp.exp(jax.random.uniform(jax.random.fold_in(own, axis_at), (blocks,), jnp.float32, low / len(shards), top_value / len(shards)))
        gain = gain * jnp.repeat(steps, dims[axis_at] // blocks).reshape([-1 if axis == axis_at else 1 for axis in range(len(dims))])
    return gain


def centred(key, dims, spread, bound, shards=(), dtype=jnp.bfloat16):
    gain = steps_of(key, dims, shards, -0.22, 0.18) if shards else 1.0
    drawn = jax.random.normal(key, dims, jnp.float32) * spread * gain
    return jnp.minimum(jnp.maximum(drawn, -bound), bound).astype(dtype)


def setup_inputs(seed: int = 0) -> dict:
    key_list = jax.random.split(jax.random.key(seed), 6)
    return {
        "tokens": draw_tokens(jax.random.fold_in(key_list[5], 71), 0),
        "norm_gains": jnp.clip(1.0 + 0.1 * jax.random.normal(key_list[1], (LAYERS, D), jnp.float32), 0.5, 1.5),
        "qkv_weight": draw_qkv_weight(jax.random.fold_in(key_list[5], 71), 0),
        "out_weight": centred(key_list[3], (LAYERS, D, KVH * GROUP * HD), (KVH * GROUP * HD) ** -0.5, 0.09375, ((0, 2), (1, 4), (2, 4))),
        "cotangent": centred(key_list[4], (SEQS, SEQ, D), (4.0 / (SEQ * SEQS) ** 0.5), 2.5, ((0, 4),)),
    }


EPSILON = 1e-05
HIGH = lax.Precision.HIGHEST

def norm_parts(block_rows, gain_row):
    values = block_rows.astype(jnp.float32)
    recip_rms = lax.rsqrt(lax.optimization_barrier(jnp.mean(values * values, axis=-1, keepdims=True)) + EPSILON)
    normed = values * recip_rms
    return (normed, recip_rms, (normed * gain_row.astype(jnp.float32)).astype(jnp.bfloat16))

def attend(query_rows, key_rows, value_rows, query_pos, key_pos):
    score_scale = HD ** (-0.5)
    scores = jnp.einsum('rgjd,cgd->gjrc', query_rows.astype(jnp.float32), key_rows.astype(jnp.float32), precision=HIGH) * score_scale
    allowed = key_pos[None, :] <= query_pos[:, None]
    scores = jnp.where(allowed, scores, -jnp.inf)
    row_max = lax.optimization_barrier(jnp.max(scores, axis=-1, keepdims=True))
    raised = jnp.exp(scores - row_max)
    attn_probs = raised / lax.optimization_barrier(jnp.sum(raised, axis=-1, keepdims=True))
    probs_low = attn_probs.astype(jnp.bfloat16)
    mixed_rows = jnp.einsum('gjrc,cgd->rgjd', lax.optimization_barrier(probs_low).astype(jnp.float32), value_rows.astype(jnp.float32), precision=HIGH)
    return (attn_probs, probs_low, mixed_rows.astype(jnp.bfloat16))

def attend_back(query_rows, key_rows, value_rows, attn_probs, probs_low, grad_mixed):
    score_scale = HD ** (-0.5)
    grad_float = grad_mixed.astype(jnp.float32)
    grad_low = jnp.einsum('rgjd,cgd->gjrc', grad_float, value_rows.astype(jnp.float32), precision=HIGH)
    inner_sum = lax.optimization_barrier(jnp.sum(attn_probs * grad_low, axis=-1, keepdims=True))
    grad_score = attn_probs * (grad_low - inner_sum) * score_scale
    grad_query = jnp.einsum('gjrc,cgd->rgjd', grad_score, key_rows.astype(jnp.float32), precision=HIGH)
    grad_key = jnp.einsum('gjrc,rgjd->cgd', grad_score, query_rows.astype(jnp.float32), precision=HIGH)
    grad_value = jnp.einsum('gjrc,rgjd->cgd', probs_low.astype(jnp.float32), grad_float, precision=HIGH)
    return (grad_query, grad_key, grad_value)

def layer_forward(layer_in, gain_row, qkv_mat, out_mat):
    normed, recip_rms, normed_low = norm_parts(layer_in, gain_row)
    projected = jnp.dot(normed_low, qkv_mat, preferred_element_type=jnp.float32).reshape(SEQ, KVH, GROUP + 2, HD)
    query_rows = projected[:, :, :GROUP].astype(jnp.bfloat16)
    key_rows = projected[:, :, GROUP].astype(jnp.bfloat16)
    value_rows = projected[:, :, GROUP + 1].astype(jnp.bfloat16)
    positions = jnp.arange(SEQ)
    attn_probs, probs_low, mixed_rows = attend(query_rows, key_rows, value_rows, positions, positions)
    flat_mixed = mixed_rows.reshape(SEQ, KVH * GROUP * HD)
    summed = lax.dot_general(flat_mixed, out_mat, (((1,), (1,)), ((), ())), preferred_element_type=jnp.float32)
    layer_out = (layer_in.astype(jnp.float32) + summed).astype(jnp.bfloat16)
    return (layer_out, (normed, recip_rms, normed_low, query_rows, key_rows, value_rows, attn_probs, probs_low, flat_mixed))

def layer_backward(grad_out, gain_row, qkv_mat, out_mat, saved):
    normed, recip_rms, normed_low, query_rows, key_rows, value_rows, attn_probs, probs_low, flat_mixed = saved
    grad_mixed = jnp.dot(grad_out, out_mat, preferred_element_type=jnp.float32).astype(jnp.bfloat16).reshape(SEQ, KVH, GROUP, HD)
    grad_query, grad_key, grad_value = attend_back(query_rows, key_rows, value_rows, attn_probs, probs_low, grad_mixed)
    grad_proj = jnp.concatenate([grad_query.astype(jnp.bfloat16), grad_key.astype(jnp.bfloat16)[:, :, None], grad_value.astype(jnp.bfloat16)[:, :, None]], axis=2).reshape(SEQ, KVH * (GROUP + 2) * HD)
    grad_normed = lax.dot_general(grad_proj, qkv_mat, (((1,), (1,)), ((), ())), preferred_element_type=jnp.float32).astype(jnp.bfloat16)
    grad_float = grad_normed.astype(jnp.float32)
    scaled = grad_float * gain_row.astype(jnp.float32)
    grad_norm_in = recip_rms * (scaled - normed * lax.optimization_barrier(jnp.mean(scaled * normed, axis=-1, keepdims=True)))
    grad_in = (grad_out.astype(jnp.float32) + grad_norm_in).astype(jnp.bfloat16)
    part_qkv = lax.dot_general(normed_low, grad_proj, (((0,), (0,)), ((), ())), preferred_element_type=jnp.float32)
    part_out = lax.dot_general(grad_out, flat_mixed, (((0,), (0,)), ((), ())), preferred_element_type=jnp.float32)
    part_gain = lax.optimization_barrier(jnp.sum(grad_float * normed, axis=0))
    return (grad_in, part_qkv, part_out, part_gain)

def merge_parts(parts):
    return lax.optimization_barrier(jnp.sum(lax.optimization_barrier(parts.astype(jnp.bfloat16)).astype(jnp.float32), axis=0))

def reference(tokens, norm_gains, qkv_weight, out_weight, cotangent):
    forward = jax.vmap(layer_forward, in_axes=(0, None, None, None))
    backward = jax.vmap(layer_backward, in_axes=(0, None, None, None, 0))
    hidden_rows = tokens
    saved_layers = []
    for layer_index in range(LAYERS):
        hidden_rows, saved = forward(hidden_rows, norm_gains[layer_index], qkv_weight[layer_index], out_weight[layer_index])
        saved_layers.append(saved)
    flowing = cotangent
    qkv_list = [None] * LAYERS
    out_list = [None] * LAYERS
    gain_list = [None] * LAYERS
    for layer_index in reversed(range(LAYERS)):
        flowing, part_qkv, part_out, part_gain = backward(flowing, norm_gains[layer_index], qkv_weight[layer_index], out_weight[layer_index], saved_layers[layer_index])
        qkv_list[layer_index] = merge_parts(part_qkv)
        out_list[layer_index] = merge_parts(part_out)
        gain_list[layer_index] = merge_parts(part_gain)
    return (jnp.stack(qkv_list), jnp.stack(out_list), jnp.stack(gain_list))
```

```python
import functools

import jax
import jax.numpy as jnp
from jax import lax
from jax.experimental import pallas as pl
from jax.experimental.pallas import tpu as pltpu
from jax.sharding import PartitionSpec as P

HD = 128
GROUP = 4
EPSILON = 1e-05
BF = jnp.bfloat16
F32 = jnp.float32
MESH = pl.DeviceIdType.MESH
KERNELS = True


def dot(a, b, ca, cb):
    return lax.dot_general(a, b, (((ca,), (cb,)), ((), ())), preferred_element_type=F32)


def exchange_kernel(axis, spread, count, *refs):
    arrays = len(spread)
    ins, outs = refs[:arrays], refs[arrays : 2 * arrays]
    send_sems, recv_sems, own_sems = refs[2 * arrays :]
    me = lax.axis_index(axis)
    barrier = pltpu.get_barrier_semaphore()
    for step in range(1, count):
        peer = lax.rem(me + step, count)
        pl.semaphore_signal(barrier, inc=1, device_id={axis: peer}, device_id_type=MESH)
    own = []
    for index in range(arrays):
        block = ins[index].at[me] if spread[index] else ins[index]
        copy = pltpu.make_async_copy(block, outs[index].at[me], own_sems.at[index])
        copy.start()
        own.append(copy)
    pl.semaphore_wait(barrier, count - 1)
    sent = []
    for step in range(1, count):
        peer = lax.rem(me + step, count)
        for index in range(arrays):
            copy = pltpu.make_async_remote_copy(
                src_ref=ins[index].at[peer] if spread[index] else ins[index],
                dst_ref=outs[index].at[me],
                send_sem=send_sems.at[index, step],
                recv_sem=recv_sems.at[index, step],
                device_id={axis: peer},
                device_id_type=MESH,
            )
            copy.start()
            sent.append(copy)
    for copy in own:
        copy.wait()
    for copy in sent:
        copy.wait()


def exchange(axis, arrays, spread, collective_id):
    if not KERNELS:
        return [
            lax.all_to_all(a, axis, 0, 0) if s else lax.all_gather(a, axis) for a, s in zip(arrays, spread)
        ]
    count = lax.axis_size(axis)
    shapes = [a.shape if s else (count, *a.shape) for a, s in zip(arrays, spread)]
    vmem = pl.BlockSpec(memory_space=pltpu.VMEM)
    return pl.pallas_call(
        functools.partial(exchange_kernel, axis, spread, count),
        out_shape=[jax.ShapeDtypeStruct(s, a.dtype) for s, a in zip(shapes, arrays)],
        in_specs=[vmem] * len(arrays),
        out_specs=[vmem] * len(arrays),
        scratch_shapes=[
            pltpu.SemaphoreType.DMA((len(arrays), count)),
            pltpu.SemaphoreType.DMA((len(arrays), count)),
            pltpu.SemaphoreType.DMA((len(arrays),)),
        ],
        compiler_params=pltpu.CompilerParams(
            collective_id=collective_id, has_side_effects=True, vmem_limit_bytes=48 << 20
        ),
    )(*arrays)


def relay_kernel(count, part_ref, rest_ref, out_ref, landed, own, passed, sems, pipe_sems, gather_sems):
    tensor = lax.axis_index("tensor")
    other = 1 - lax.axis_index("pipe")
    barrier = pltpu.get_barrier_semaphore()
    for step in range(1, count):
        peer = lax.rem(tensor + step, count)
        pl.semaphore_signal(barrier, inc=1, device_id={"tensor": peer}, device_id_type=MESH)
    pl.semaphore_signal(barrier, inc=1, device_id={"pipe": other}, device_id_type=MESH)
    pl.semaphore_wait(barrier, count)
    copies = []
    for step in range(1, count):
        peer = lax.rem(tensor + step, count)
        copy = pltpu.make_async_remote_copy(
            src_ref=part_ref.at[peer],
            dst_ref=landed.at[step],
            send_sem=sems.at[0, step],
            recv_sem=sems.at[1, step],
            device_id={"tensor": peer},
            device_id_type=MESH,
        )
        copy.start()
        copies.append(copy)
    total = rest_ref[...].astype(F32) + part_ref[tensor].astype(F32)
    for step, copy in enumerate(copies, 1):
        copy.wait_recv()
        total = total + landed[step].astype(F32)
    own[...] = total.astype(BF)
    across = pltpu.make_async_remote_copy(
        src_ref=own,
        dst_ref=passed,
        send_sem=pipe_sems.at[0],
        recv_sem=pipe_sems.at[1],
        device_id={"pipe": other},
        device_id_type=MESH,
    )
    across.start()
    across.wait_recv()
    spread = []
    for step in range(1, count):
        peer = lax.rem(tensor + step, count)
        copy = pltpu.make_async_remote_copy(
            src_ref=passed,
            dst_ref=out_ref.at[tensor],
            send_sem=gather_sems.at[0, step],
            recv_sem=gather_sems.at[1, step],
            device_id={"tensor": peer},
            device_id_type=MESH,
        )
        copy.start()
        spread.append(copy)
    out_ref[tensor] = passed[...]
    for copy in copies:
        copy.wait_send()
    across.wait_send()
    for copy in spread:
        copy.wait()


def relay(parts, rest, collective_id):
    count = lax.axis_size("tensor")
    rows, width = parts.shape[0] // count, parts.shape[1]
    parts = parts.reshape(count, rows, width)
    own = lax.dynamic_index_in_dim(rest.reshape(count, rows, width), lax.axis_index("tensor"), 0, False)
    if not KERNELS:
        summed = lax.psum_scatter(parts, "tensor", scatter_dimension=0, tiled=False).astype(F32)
        passed = lax.ppermute((own.astype(F32) + summed).astype(BF), "pipe", [(0, 1), (1, 0)])
        return lax.all_gather(passed, "tensor").reshape(count * rows, width)
    vmem = pl.BlockSpec(memory_space=pltpu.VMEM)
    out = pl.pallas_call(
        functools.partial(relay_kernel, count),
        out_shape=jax.ShapeDtypeStruct(parts.shape, BF),
        in_specs=[vmem] * 2,
        out_specs=vmem,
        scratch_shapes=[
            pltpu.VMEM(parts.shape, BF),
            pltpu.VMEM((rows, width), BF),
            pltpu.VMEM((rows, width), BF),
            pltpu.SemaphoreType.DMA((2, count)),
            pltpu.SemaphoreType.DMA((2,)),
            pltpu.SemaphoreType.DMA((2, count)),
        ],
        compiler_params=pltpu.CompilerParams(
            collective_id=collective_id, has_side_effects=True, vmem_limit_bytes=48 << 20
        ),
    )(parts, own)
    return out.reshape(count * rows, width)


def split_heads(flat, seq, groups, count):
    return jnp.transpose(flat.reshape(seq, groups, count, HD), (1, 2, 0, 3))


def attend(proj, seq, groups):
    heads = split_heads(proj, seq, groups, GROUP + 2)
    query = heads[:, :GROUP].reshape(groups, GROUP * seq, HD)
    key, value = heads[:, GROUP], heads[:, GROUP + 1]
    scores = jnp.einsum("grd,gcd->grc", query, key, preferred_element_type=F32) * HD**-0.5
    scores = scores.reshape(groups, GROUP, seq, seq)
    scores = jnp.where(jnp.tri(seq, dtype=bool), scores, -jnp.inf)
    raised = jnp.exp(scores - jnp.max(scores, axis=-1, keepdims=True))
    probs = (raised / jnp.sum(raised, axis=-1, keepdims=True)).reshape(groups, GROUP * seq, seq)
    mixed = jnp.einsum("grc,gcd->grd", probs.astype(BF), value, preferred_element_type=F32)
    mixed = mixed.astype(BF).reshape(groups, GROUP, seq, HD)
    return query, key, value, probs, jnp.transpose(mixed, (2, 0, 1, 3)).reshape(seq, groups * GROUP * HD)


def attend_back(query, key, value, probs, grad_mixed, seq, groups):
    grad = split_heads(grad_mixed, seq, groups, GROUP).reshape(groups, GROUP * seq, HD)
    grad_low = jnp.einsum("grd,gcd->grc", grad, value, preferred_element_type=F32)
    inner = jnp.sum(probs * grad_low, axis=-1, keepdims=True)
    grad_score = (probs * (grad_low - inner) * HD**-0.5).astype(BF)
    grad_query = jnp.einsum("grc,gcd->grd", grad_score, key, preferred_element_type=F32)
    grad_key = jnp.einsum("grc,grd->gcd", grad_score, query, preferred_element_type=F32)
    grad_value = jnp.einsum("grc,grd->gcd", probs.astype(BF), grad, preferred_element_type=F32)
    heads = jnp.concatenate(
        [grad_query.reshape(groups, GROUP, seq, HD), grad_key[:, None], grad_value[:, None]], axis=1
    )
    return jnp.transpose(heads, (2, 0, 1, 3)).reshape(seq, groups * (GROUP + 2) * HD)


def shards(tokens, norm_gains, qkv_weight, out_weight, cotangent):
    first = lax.axis_index("pipe") == 0
    count = lax.axis_size("dp")
    qkv, out = qkv_weight[0], out_weight[0]
    width, cols = qkv.shape
    head_cols = out.shape[1]
    seq, model = tokens.shape[1:]
    rows = count * seq
    groups = cols // ((GROUP + 2) * HD)
    gain = lax.dynamic_slice_in_dim(norm_gains[0], lax.axis_index("dp") * width, width, 0)[None]

    def project(block):
        scaled = block.astype(F32)
        squares = jnp.sum(scaled * scaled, axis=-1).reshape(count, 1, seq)
        squares = jnp.broadcast_to(squares, (count, 8, seq))
        return dot((scaled * gain).astype(BF), qkv, 1, 0).astype(BF), squares

    def summed(slots):
        return jnp.sum(slots.astype(F32), axis=0)

    held = jnp.where(first, tokens[0], cotangent[0])
    held = jnp.transpose(held.reshape(seq, count, width), (1, 0, 2))
    (held,) = exchange("dp", [held], [True], 0)
    held = held.reshape(rows, width)

    proj_part, squares = project(held)
    mixed_part = dot(held, out, 1, 0).astype(BF)
    mixed_part = jnp.pad(mixed_part, ((0, 0), (0, cols - head_cols)))
    part = jnp.where(first, proj_part, mixed_part).reshape(count, seq, cols)
    part, squares = exchange("dp", [part, squares], [True, True], 1)
    raw_start = summed(part)
    squares_start = summed(squares)[0]
    recip = lax.rsqrt(squares_start / model + EPSILON)[:, None]
    grad_mixed_start = raw_start[:, :head_cols].astype(BF)
    mixed = attend((raw_start * recip).astype(BF), seq, groups)[-1]
    (mixed_start,) = exchange("dp", [mixed], [False], 2)
    mixed_start = mixed_start.reshape(rows, head_cols)
    carried = relay(dot(mixed_start, out, 1, 1).astype(BF), held, 3)

    part, squares = project(carried)
    part, squares = exchange("dp", [part.reshape(count, seq, cols), squares], [True, True], 4)
    raw_next = summed(part)
    raw = jnp.where(first, raw_start, raw_next)
    recip = lax.rsqrt(jnp.where(first, squares_start, summed(squares)[0]) / model + EPSILON)[:, None]
    query, key, value, probs, mixed = attend((raw * recip).astype(BF), seq, groups)
    grad_proj = attend_back(query, key, value, probs, grad_mixed_start, seq, groups)
    grad_proj = (grad_proj * recip).astype(BF)
    coef = jnp.sum(grad_proj.astype(F32) * raw, axis=-1) * (recip[:, 0] * recip[:, 0]) / model
    coef = jnp.broadcast_to(coef[None], (8, seq))
    grad_proj_next, mixed_next, coef = exchange("dp", [grad_proj, mixed, coef], [False] * 3, 5)
    grad_proj_next = grad_proj_next.reshape(rows, cols)
    coef = coef[:, 0].reshape(rows, 1)
    back = dot(grad_proj_next, qkv, 1, 1) * gain - carried.astype(F32) * coef
    returned = relay(back.astype(BF), held, 6)

    part = dot(returned, out, 1, 0).astype(BF).reshape(count, seq, head_cols)
    (part,) = exchange("dp", [part], [True], 7)
    grad_proj = attend_back(query, key, value, probs, summed(part).astype(BF), seq, groups)
    grad_proj = (grad_proj * recip).astype(BF)
    (grad_proj,) = exchange("dp", [grad_proj], [False], 8)

    block_in = jnp.where(first, held, carried)
    grad_out = jnp.where(first, returned, held)
    mixed_all = jnp.where(first, mixed_start, mixed_next.reshape(rows, head_cols))
    grad_proj = jnp.where(first, grad_proj.reshape(rows, cols), grad_proj_next)
    out_grad = dot(grad_out, mixed_all, 0, 0)
    weight = dot(block_in, grad_proj, 0, 0)
    qkv_grad = weight * gain.reshape(width, 1)
    gain_grad = lax.psum(jnp.sum(weight * qkv.astype(F32), axis=-1), "tensor")
    return qkv_grad[None], out_grad[None], gain_grad[None]


def solution(mesh):
    in_specs = (
        P("dp", None, None),
        P("pipe", None),
        P("pipe", "dp", "tensor"),
        P("pipe", "dp", "tensor"),
        P("dp", None, None),
    )
    out_specs = (P("pipe", "dp", "tensor"), P("pipe", "dp", "tensor"), P("pipe", "dp"))
    return jax.shard_map(shards, mesh=mesh, in_specs=in_specs, out_specs=out_specs, check_vma=False)
```

```python
import functools

import jax
import jax.numpy as jnp
from jax import lax
from jax.experimental import pallas as pl
from jax.experimental.pallas import tpu as pltpu
from jax.sharding import PartitionSpec as P

HD = 128
GROUP = 4
EPSILON = 1e-05
BF = jnp.bfloat16
F32 = jnp.float32
MESH = pl.DeviceIdType.MESH


def dot(a, b, ca, cb):
    return lax.dot_general(a, b, (((ca,), (cb,)), ((), ())), preferred_element_type=F32)


def meet(peers):
    barrier = pltpu.get_barrier_semaphore()
    for peer in peers:
        pl.semaphore_signal(barrier, inc=1, device_id=peer, device_id_type=MESH)
    pl.semaphore_wait(barrier, len(peers))


def others(axis):
    me, count = lax.axis_index(axis), lax.axis_size(axis)
    return [lax.rem(me + step, count) for step in range(1, count)]


def push(src, dst, sems, place, peer):
    copy = pltpu.make_async_remote_copy(
        src_ref=src,
        dst_ref=dst,
        send_sem=sems.at[(0, *place)],
        recv_sem=sems.at[(1, *place)],
        device_id=peer,
        device_id_type=MESH,
    )
    copy.start()
    return copy


def beside():
    tensor = lax.axis_index("tensor")
    core, chip = lax.rem(tensor, 2), tensor // 2
    return tensor, core, chip, chip * 2 + 1 - core, (1 - chip) * 2 + core


def call(kernel, collective_id, arrays, outs, scratch):
    vmem = pl.BlockSpec(memory_space=pltpu.VMEM)
    return pl.pallas_call(
        kernel,
        out_shape=[jax.ShapeDtypeStruct(shape, dtype) for shape, dtype in outs],
        in_specs=[vmem] * len(arrays),
        out_specs=[vmem] * len(outs),
        scratch_shapes=scratch,
        compiler_params=pltpu.CompilerParams(
            collective_id=collective_id, has_side_effects=True, vmem_limit_bytes=48 << 20
        ),
    )(*arrays)


def spread_kernel(count, tokens_ref, cotangent_ref, out_ref, picked, dp_sems, chip_sems, core_sems, far_sems):
    me = lax.axis_index("dp")
    tensor, core, chip, sibling, across = beside()
    peers = others("dp")
    meet([{"dp": p} for p in peers] + [{"tensor": sibling}, {"tensor": across}])
    rows, width = picked.shape[0], out_ref.shape[2]
    mine = pl.ds(pl.multiple_of(tensor * rows, rows), rows)
    far = pl.ds(pl.multiple_of(across * rows, rows), rows)
    first = lax.axis_index("pipe") == 0
    picked[...] = jnp.where(first, tokens_ref[mine, :], cotangent_ref[mine, :])
    copies, later = [], []
    for step, peer in enumerate(peers, 1):
        block = picked.at[:, pl.ds(pl.multiple_of(peer * width, width), width)]
        copies.append(push(block, out_ref.at[me, mine], dp_sems, (step,), {"dp": peer}))
    out_ref[me, mine, :] = picked[:, pl.ds(pl.multiple_of(me * width, width), width)]
    for step in range(count):
        source = lax.rem(me + count - step, count)
        if step:
            copies[step - 1].wait_recv()
        block = out_ref.at[source, mine]
        later.append(push(block, block, chip_sems, (step,), {"tensor": across}))
        copies.append(push(block, block, core_sems, (step,), {"tensor": sibling}))
    for step in range(count):
        source = lax.rem(me + count - step, count)
        later[step].wait_recv()
        block = out_ref.at[source, far]
        copies.append(push(block, block, far_sems, (step,), {"tensor": sibling}))
    for step, copy in enumerate(copies):
        if step >= count - 1:
            copy.wait_recv()
        copy.wait_send()
    for copy in later:
        copy.wait_send()


def spread(tokens, cotangent, width, collective_id):
    count = lax.axis_size("dp")
    seq, model = tokens.shape
    dma = pltpu.SemaphoreType.DMA((2, count))
    (out,) = call(
        functools.partial(spread_kernel, count),
        collective_id,
        [tokens, cotangent],
        [((count, seq, width), BF)],
        [pltpu.VMEM((seq // lax.axis_size("tensor"), model), BF), dma, dma, dma, dma],
    )
    return out


def relay_kernel(chunks, beside_z, *refs):
    if beside_z:
        part_ref, rest_ref, extra_ref, out_ref, gathered = refs[:5]
        near, half, landed, own, core_sems, sems, dp_sems = refs[5:]
    else:
        part_ref, rest_ref, out_ref, near, half, landed, own, core_sems, sems = refs
    tensor, core, chip, sibling, across = beside()
    section = {"pipe": 1 - lax.axis_index("pipe")}
    me = lax.axis_index("dp")
    peers = others("dp") if beside_z else []
    meet([{"dp": p} for p in peers] + [{"tensor": sibling}, {"tensor": across}, section])
    sibling_to, across_to = {"tensor": sibling}, {"tensor": across}
    rows = own.shape[0] // chunks
    cut = [pl.ds(k * rows, rows) for k in range(chunks)]
    held, firsts, seconds, across_x, fans, ends = [], [], [], [], [], []
    for k in range(chunks):
        give = (1 - chip) * 2 + 1 - core
        firsts.append(push(part_ref.at[give, cut[k]], near.at[0, cut[k]], core_sems, (0, k), sibling_to))
    for k in range(chunks):
        held.append(push(part_ref.at[sibling, cut[k]], near.at[1, cut[k]], core_sems, (1, k), sibling_to))
    for step, peer in enumerate(peers, 1):
        seconds.append(push(extra_ref, gathered.at[me], dp_sems, (step,), {"dp": peer}))
    if beside_z:
        gathered[me] = extra_ref[...]
    outs = []
    for k in range(chunks):
        firsts[k].wait_recv()
        half[cut[k], :] = (part_ref[across, cut[k], :].astype(F32) + near[0, cut[k], :].astype(F32)).astype(BF)
        outs.append(push(half.at[cut[k]], landed.at[cut[k]], sems, (0, k), across_to))
    for k in range(chunks):
        held[k].wait_recv()
        total = rest_ref[cut[k], :].astype(F32) + part_ref[tensor, cut[k], :].astype(F32)
        total = total + near[1, cut[k], :].astype(F32)
        outs[k].wait_recv()
        own[cut[k], :] = (total + landed[cut[k], :].astype(F32)).astype(BF)
        across_x.append(push(own.at[cut[k]], out_ref.at[tensor, cut[k]], sems, (1, k), section))
    for k in range(chunks):
        across_x[k].wait_recv()
        block = out_ref.at[tensor, cut[k]]
        fans.append(push(block, block, sems, (2, k), across_to))
        ends.append(push(block, block, core_sems, (2, k), sibling_to))
    for k in range(chunks):
        fans[k].wait_recv()
        block = out_ref.at[across, cut[k]]
        ends.append(push(block, block, core_sems, (3, k), sibling_to))
    for copy in ends + seconds:
        copy.wait_recv()
    for copy in firsts + held + outs + across_x + fans + ends + seconds:
        copy.wait_send()


def relay(parts, rest, collective_id, extra=None):
    count, dp = lax.axis_size("tensor"), lax.axis_size("dp")
    rows, width = parts.shape[0] // count, parts.shape[1]
    chunks = 4
    parts = parts.reshape(count, rows, width)
    own = lax.dynamic_index_in_dim(rest.reshape(count, rows, width), lax.axis_index("tensor"), 0, False)
    more = [] if extra is None else [extra]
    block = pltpu.VMEM((rows, width), BF)
    results = call(
        functools.partial(relay_kernel, chunks, bool(more)),
        collective_id,
        [parts, own] + more,
        [(parts.shape, BF)] + [((dp, *a.shape), a.dtype) for a in more],
        [
            pltpu.VMEM((2, rows, width), BF),
            block,
            block,
            block,
            pltpu.SemaphoreType.DMA((2, 4, chunks)),
            pltpu.SemaphoreType.DMA((2, 3, chunks)),
        ]
        + [pltpu.SemaphoreType.DMA((2, dp)) for a in more],
    )
    out = results[0].reshape(count * rows, width)
    return (out, results[1]) if more else out


def column(row):
    size = row.shape[1]
    same = lax.broadcasted_iota(jnp.int32, (size, size), 0) == lax.broadcasted_iota(jnp.int32, (size, size), 1)
    return jnp.sum(jnp.where(same, row, 0.0), axis=1, keepdims=True)


def as_row(col):
    size = col.shape[0]
    same = lax.broadcasted_iota(jnp.int32, (size, size), 0) == lax.broadcasted_iota(jnp.int32, (size, size), 1)
    return jnp.sum(jnp.where(same, col, 0.0), axis=0, keepdims=True)


def head(index):
    return pl.ds(index * HD, HD)


def probs_of(query, key):
    seq = query.shape[0]
    scores = dot(query, key, 1, 1) * HD**-0.5
    allowed = lax.broadcasted_iota(jnp.int32, (seq, seq), 1) <= lax.broadcasted_iota(jnp.int32, (seq, seq), 0)
    scores = jnp.where(allowed, scores, -jnp.inf)
    raised = jnp.exp(scores - jnp.max(scores, axis=-1, keepdims=True))
    return raised / jnp.sum(raised, axis=-1, keepdims=True)


def stage_kernel(mode, count, model, *refs):
    if mode == "forward":
        part, stat, raw_out, proj, stat_out, result, landed, stats, scatter, gather, small = refs
    elif mode == "both":
        part, stat, grads, result, coef_out, mixed_out, landed, stats, proj, scatter, gather, small = refs
    else:
        part, proj, stat, result, landed, probs_all, scatter, gather = refs
    me = lax.axis_index("dp")
    peers = others("dp")
    meet([{"dp": p} for p in peers])
    groups = scatter.shape[1]
    seq = part.shape[1]
    cols = part.shape[2] // groups
    full = (GROUP + 2) * HD
    low = GROUP * HD
    copies, arrivals, ends, stat_copies = [], [], [], []
    if mode != "backward":
        for step, peer in enumerate(peers, 1):
            stat_copies.append(push(stat.at[peer], stats.at[step], small, (0, step), {"dp": peer}))
    for g in range(groups):
        strip = pl.ds(g * cols, cols)
        arrivals.append(
            [
                push(part.at[peer, :, strip], landed.at[step, :, strip], scatter, (g, step), {"dp": peer})
                for step, peer in enumerate(peers, 1)
            ]
        )
    if mode == "backward":
        recip = lax.rsqrt(column(stat[0:1, :]) / model + EPSILON)
        for g in range(groups):
            for j in range(GROUP):
                query, key = proj[:, head(g * (GROUP + 2) + j)], proj[:, head(g * (GROUP + 2) + GROUP)]
                probs_all[g * GROUP + j] = probs_of(query, key)
    else:
        squares = stat[me]
        for step, copy in enumerate(stat_copies, 1):
            copy.wait_recv()
            squares = squares + stats[step]
        recip = lax.rsqrt(column(squares[0:1, :]) / model + EPSILON)
        if mode == "forward":
            stat_out[...] = squares
    coef = jnp.zeros((seq, 1), F32)
    for g in range(groups):
        base = g * full
        for copy in arrivals[g]:
            copy.wait_recv()

        def total(at):
            sums = part[me, :, at].astype(F32)
            for step in range(1, count):
                sums = sums + landed[step, :, at].astype(F32)
            return sums

        if mode != "backward":
            for i in range(GROUP + 2):
                at = pl.ds(base + i * HD, HD)
                raw = total(at)
                if mode == "forward":
                    raw_out[:, at] = raw.astype(BF)
                proj[:, at] = (raw * recip).astype(BF)
        key, value = proj[:, pl.ds(base + low, HD)], proj[:, pl.ds(base + low + HD, HD)]
        grad_key = jnp.zeros((seq, HD), F32)
        grad_value = jnp.zeros((seq, HD), F32)
        for j in range(GROUP):
            at = pl.ds(base + j * HD, HD)
            mixed_at = pl.ds(g * low + j * HD, HD)
            query = proj[:, at]
            probs = probs_all[g * GROUP + j] if mode == "backward" else probs_of(query, key)
            probs_low = probs.astype(BF)
            if mode != "backward":
                mixed = dot(probs_low, value, 1, 0).astype(BF)
            if mode == "forward":
                result[me, :, mixed_at] = mixed
                continue
            if mode == "both":
                mixed_out[:, mixed_at] = mixed
                grad = grads[:, mixed_at]
            else:
                grad = total(mixed_at).astype(BF)
            grad_low = dot(grad, value, 1, 1)
            inner = jnp.sum(probs * grad_low, axis=-1, keepdims=True)
            grad_score = (probs * (grad_low - inner) * HD**-0.5).astype(BF)
            grad_query = dot(grad_score, key, 1, 0)
            grad_key = grad_key + dot(grad_score, query, 0, 0)
            grad_value = grad_value + dot(probs_low, grad, 0, 0)
            result[me, :, at] = (grad_query * recip).astype(BF)
            if mode == "both":
                coef = coef + jnp.sum(grad_query * query.astype(F32), axis=-1, keepdims=True)
        if mode == "forward":
            strip = pl.ds(g * low, low)
        else:
            strip = pl.ds(base, full)
            result[me, :, pl.ds(base + low, HD)] = (grad_key * recip).astype(BF)
            result[me, :, pl.ds(base + low + HD, HD)] = (grad_value * recip).astype(BF)
            if mode == "both":
                coef = coef + jnp.sum(grad_key * key.astype(F32), axis=-1, keepdims=True)
                coef = coef + jnp.sum(grad_value * value.astype(F32), axis=-1, keepdims=True)
        for step, peer in enumerate(peers, 1):
            block = result.at[me, :, strip]
            ends.append(push(block, block, gather, (g, step), {"dp": peer}))
    if mode == "both":
        coef_out[me] = jnp.broadcast_to(as_row(coef * recip * recip / model), coef_out.shape[1:])
        for step, peer in enumerate(peers, 1):
            block = coef_out.at[me]
            ends.append(push(block, block, small, (1, step), {"dp": peer}))
    for copy in ends:
        copy.wait()
    for copy in sum(arrivals, stat_copies):
        copy.wait_send()


def stage(mode, arrays, groups, model, collective_id):
    part = arrays[0]
    count, seq, cols = part.shape
    full = groups * (GROUP + 2) * HD
    low = groups * GROUP * HD
    dma = pltpu.SemaphoreType.DMA
    sems = [dma((2, groups, count)), dma((2, groups, count))]
    landed = pltpu.VMEM(part.shape, BF)
    if mode == "backward":
        outs = [((count, seq, full), BF)]
        scratch = [landed, pltpu.VMEM((groups * GROUP, seq, seq), F32), *sems]
    else:
        stats = pltpu.VMEM((count, 8, seq), F32)
        if mode == "forward":
            outs = [((seq, full), BF), ((seq, full), BF), ((8, seq), F32), ((count, seq, low), BF)]
            scratch = [landed, stats, *sems, dma((2, 2, count))]
        else:
            outs = [((count, seq, full), BF), ((count, 8, seq), F32), ((seq, low), BF)]
            scratch = [landed, stats, pltpu.VMEM((seq, full), BF), *sems, dma((2, 2, count))]
    return call(functools.partial(stage_kernel, mode, count, model), collective_id, arrays, outs, scratch)


def total_kernel(count, in_ref, out_ref, landed, sems):
    meet([{"tensor": p} for p in others("tensor")])
    copies = [
        push(in_ref, landed.at[step], sems, (step,), {"tensor": peer})
        for step, peer in enumerate(others("tensor"), 1)
    ]
    total = in_ref[...]
    for step, copy in enumerate(copies, 1):
        copy.wait_recv()
        total = total + landed[step]
    out_ref[...] = total
    for copy in copies:
        copy.wait_send()


def tensor_total(array, collective_id):
    count = lax.axis_size("tensor")
    scratch = [pltpu.VMEM((count, *array.shape), F32), pltpu.SemaphoreType.DMA((2, count))]
    return call(functools.partial(total_kernel, count), collective_id, [array], [(array.shape, F32)], scratch)[0]


def shards(tokens, norm_gains, qkv_weight, out_weight, cotangent):
    first = lax.axis_index("pipe") == 0
    count = lax.axis_size("dp")
    qkv, out = qkv_weight[0], out_weight[0]
    width, cols = qkv.shape
    head_cols = out.shape[1]
    seq, model = tokens.shape[1:]
    rows = count * seq
    groups = cols // ((GROUP + 2) * HD)
    gain = lax.dynamic_slice_in_dim(norm_gains[0], lax.axis_index("dp") * width, width, 0)[None]

    def project(block):
        scaled = block.astype(F32)
        squares = jnp.sum(scaled * scaled, axis=-1).reshape(count, 1, seq)
        squares = jnp.broadcast_to(squares, (count, 8, seq))
        return dot((scaled * gain).astype(BF), qkv, 1, 0).astype(BF), squares

    held = spread(tokens[0], cotangent[0], width, 0).reshape(rows, width)

    proj_part, squares = project(held)
    mixed_part = jnp.pad(dot(held, out, 1, 0).astype(BF), ((0, 0), (0, cols - head_cols)))
    part = jnp.where(first, proj_part, mixed_part).reshape(count, seq, cols)
    grads, proj, squares, mixed_start = stage("forward", [part, squares], groups, model, 1)
    mixed_start = mixed_start.reshape(rows, head_cols)
    carried = relay(dot(mixed_start, out, 1, 1).astype(BF), held, 2)

    part, next_squares = project(carried)
    part = part.reshape(count, seq, cols)
    grad_proj_next, coef, mixed = stage("both", [part, next_squares, grads], groups, model, 3)
    grad_proj_next = grad_proj_next.reshape(rows, cols)
    coef = coef[:, 0].reshape(rows, 1)
    back = dot(grad_proj_next, qkv, 1, 1) * gain - carried.astype(F32) * coef
    returned, mixed_next = relay(back.astype(BF), held, 4, mixed)

    part = dot(returned, out, 1, 0).astype(BF).reshape(count, seq, head_cols)
    (grad_proj,) = stage("backward", [part, proj, squares], groups, model, 5)

    block_in = jnp.where(first, held, carried)
    grad_out = jnp.where(first, returned, held)
    mixed_all = jnp.where(first, mixed_start, mixed_next.reshape(rows, head_cols))
    grad_proj = jnp.where(first, grad_proj.reshape(rows, cols), grad_proj_next)
    out_grad = dot(grad_out, mixed_all, 0, 0)
    weight = dot(block_in, grad_proj, 0, 0)
    qkv_grad = weight * gain.reshape(width, 1)
    gain_part = jnp.sum(weight * qkv.astype(F32), axis=-1)
    gain_grad = tensor_total(gain_part.reshape(width // 128, 128), 6).reshape(1, width)
    return qkv_grad[None], out_grad[None], gain_grad


def solution(mesh):
    in_specs = (
        P("dp", None, None),
        P("pipe", None),
        P("pipe", "dp", "tensor"),
        P("pipe", "dp", "tensor"),
        P("dp", None, None),
    )
    out_specs = (P("pipe", "dp", "tensor"), P("pipe", "dp", "tensor"), P("pipe", "dp"))
    return jax.shard_map(shards, mesh=mesh, in_specs=in_specs, out_specs=out_specs, check_vma=False)
```

```python
import functools

import jax
import jax.numpy as jnp
from jax import lax
from jax.experimental import pallas as pl
from jax.experimental.pallas import tpu as pltpu
from jax.sharding import PartitionSpec as P

HD = 128
GROUP = 4
EPSILON = 1e-05
BF = jnp.bfloat16
F32 = jnp.float32
MESH = pl.DeviceIdType.MESH


def dot(a, b, ca, cb):
    return lax.dot_general(a, b, (((ca,), (cb,)), ((), ())), preferred_element_type=F32)


def meet(peers):
    barrier = pltpu.get_barrier_semaphore()
    for peer in peers:
        pl.semaphore_signal(barrier, inc=1, device_id=peer, device_id_type=MESH)
    pl.semaphore_wait(barrier, len(peers))


def others(axis):
    me, count = lax.axis_index(axis), lax.axis_size(axis)
    return [lax.rem(me + step, count) for step in range(1, count)]


def push(src, dst, sems, place, peer):
    copy = pltpu.make_async_remote_copy(
        src_ref=src,
        dst_ref=dst,
        send_sem=sems.at[(0, *place)],
        recv_sem=sems.at[(1, *place)],
        device_id=peer,
        device_id_type=MESH,
    )
    copy.start()
    return copy


def beside():
    tensor = lax.axis_index("tensor")
    core, chip = lax.rem(tensor, 2), tensor // 2
    return tensor, core, chip, chip * 2 + 1 - core, (1 - chip) * 2 + core


def call(kernel, collective_id, arrays, outs, scratch):
    vmem = pl.BlockSpec(memory_space=pltpu.VMEM)
    return pl.pallas_call(
        kernel,
        out_shape=[jax.ShapeDtypeStruct(shape, dtype) for shape, dtype in outs],
        in_specs=[vmem] * len(arrays),
        out_specs=[vmem] * len(outs),
        scratch_shapes=scratch,
        compiler_params=pltpu.CompilerParams(
            collective_id=collective_id, has_side_effects=True, vmem_limit_bytes=48 << 20
        ),
    )(*arrays)


def spread_kernel(count, tokens_ref, cotangent_ref, out_ref, picked, dp_sems, chip_sems, core_sems, far_sems):
    me = lax.axis_index("dp")
    tensor, core, chip, sibling, across = beside()
    peers = others("dp")
    meet([{"dp": p} for p in peers] + [{"tensor": sibling}, {"tensor": across}])
    rows, width = picked.shape[0], out_ref.shape[2]
    mine = pl.ds(pl.multiple_of(tensor * rows, rows), rows)
    far = pl.ds(pl.multiple_of(across * rows, rows), rows)
    first = lax.axis_index("pipe") == 0
    picked[...] = jnp.where(first, tokens_ref[mine, :], cotangent_ref[mine, :])
    copies, later = [], []
    for step, peer in enumerate(peers, 1):
        block = picked.at[:, pl.ds(pl.multiple_of(peer * width, width), width)]
        copies.append(push(block, out_ref.at[me, mine], dp_sems, (step,), {"dp": peer}))
    out_ref[me, mine, :] = picked[:, pl.ds(pl.multiple_of(me * width, width), width)]
    for step in range(count):
        source = lax.rem(me + count - step, count)
        if step:
            copies[step - 1].wait_recv()
        block = out_ref.at[source, mine]
        later.append(push(block, block, chip_sems, (step,), {"tensor": across}))
        copies.append(push(block, block, core_sems, (step,), {"tensor": sibling}))
    for step in range(count):
        source = lax.rem(me + count - step, count)
        later[step].wait_recv()
        block = out_ref.at[source, far]
        copies.append(push(block, block, far_sems, (step,), {"tensor": sibling}))
    for step, copy in enumerate(copies):
        if step >= count - 1:
            copy.wait_recv()
        copy.wait_send()
    for copy in later:
        copy.wait_send()


def spread(tokens, cotangent, width, collective_id):
    count = lax.axis_size("dp")
    seq, model = tokens.shape
    dma = pltpu.SemaphoreType.DMA((2, count))
    (out,) = call(
        functools.partial(spread_kernel, count),
        collective_id,
        [tokens, cotangent],
        [((count, seq, width), BF)],
        [pltpu.VMEM((seq // lax.axis_size("tensor"), model), BF), dma, dma, dma, dma],
    )
    return out


def relay_kernel(chunks, beside_z, *refs):
    if beside_z:
        part_ref, rest_ref, extra_ref, out_ref, gathered = refs[:5]
        near, half, landed, own, core_sems, sems, dp_sems = refs[5:]
    else:
        part_ref, rest_ref, out_ref, near, half, landed, own, core_sems, sems = refs
    tensor, core, chip, sibling, across = beside()
    section = {"pipe": 1 - lax.axis_index("pipe")}
    me = lax.axis_index("dp")
    peers = others("dp") if beside_z else []
    meet([{"dp": p} for p in peers] + [{"tensor": sibling}, {"tensor": across}, section])
    sibling_to, across_to = {"tensor": sibling}, {"tensor": across}
    rows = own.shape[0] // chunks
    cut = [pl.ds(k * rows, rows) for k in range(chunks)]
    held, firsts, seconds, across_x, fans, ends = [], [], [], [], [], []
    for k in range(chunks):
        give = (1 - chip) * 2 + 1 - core
        firsts.append(push(part_ref.at[give, cut[k]], near.at[0, cut[k]], core_sems, (0, k), sibling_to))
    for k in range(chunks):
        held.append(push(part_ref.at[sibling, cut[k]], near.at[1, cut[k]], core_sems, (1, k), sibling_to))
    for step, peer in enumerate(peers, 1):
        seconds.append(push(extra_ref, gathered.at[me], dp_sems, (step,), {"dp": peer}))
    if beside_z:
        gathered[me] = extra_ref[...]
    outs = []
    for k in range(chunks):
        firsts[k].wait_recv()
        half[cut[k], :] = (part_ref[across, cut[k], :].astype(F32) + near[0, cut[k], :].astype(F32)).astype(BF)
        outs.append(push(half.at[cut[k]], landed.at[cut[k]], sems, (0, k), across_to))
    for k in range(chunks):
        held[k].wait_recv()
        total = rest_ref[cut[k], :].astype(F32) + part_ref[tensor, cut[k], :].astype(F32)
        total = total + near[1, cut[k], :].astype(F32)
        outs[k].wait_recv()
        own[cut[k], :] = (total + landed[cut[k], :].astype(F32)).astype(BF)
        across_x.append(push(own.at[cut[k]], out_ref.at[tensor, cut[k]], sems, (1, k), section))
    for k in range(chunks):
        across_x[k].wait_recv()
        block = out_ref.at[tensor, cut[k]]
        fans.append(push(block, block, sems, (2, k), across_to))
        ends.append(push(block, block, core_sems, (2, k), sibling_to))
    for k in range(chunks):
        fans[k].wait_recv()
        block = out_ref.at[across, cut[k]]
        ends.append(push(block, block, core_sems, (3, k), sibling_to))
    for copy in ends + seconds:
        copy.wait_recv()
    for copy in firsts + held + outs + across_x + fans + ends + seconds:
        copy.wait_send()


def relay(parts, rest, collective_id, extra=None):
    count, dp = lax.axis_size("tensor"), lax.axis_size("dp")
    rows, width = parts.shape[0] // count, parts.shape[1]
    chunks = 4
    parts = parts.reshape(count, rows, width)
    own = lax.dynamic_index_in_dim(rest.reshape(count, rows, width), lax.axis_index("tensor"), 0, False)
    more = [] if extra is None else [extra]
    block = pltpu.VMEM((rows, width), BF)
    results = call(
        functools.partial(relay_kernel, chunks, bool(more)),
        collective_id,
        [parts, own] + more,
        [(parts.shape, BF)] + [((dp, *a.shape), a.dtype) for a in more],
        [
            pltpu.VMEM((2, rows, width), BF),
            block,
            block,
            block,
            pltpu.SemaphoreType.DMA((2, 4, chunks)),
            pltpu.SemaphoreType.DMA((2, 3, chunks)),
        ]
        + [pltpu.SemaphoreType.DMA((2, dp)) for a in more],
    )
    out = results[0].reshape(count * rows, width)
    return (out, results[1]) if more else out


def column(row):
    size = row.shape[1]
    same = lax.broadcasted_iota(jnp.int32, (size, size), 0) == lax.broadcasted_iota(jnp.int32, (size, size), 1)
    return jnp.sum(jnp.where(same, row, 0.0), axis=1, keepdims=True)


def as_row(col):
    size = col.shape[0]
    same = lax.broadcasted_iota(jnp.int32, (size, size), 0) == lax.broadcasted_iota(jnp.int32, (size, size), 1)
    return jnp.sum(jnp.where(same, col, 0.0), axis=0, keepdims=True)


def head(index):
    return pl.ds(index * HD, HD)


def probs_of(query, key):
    seq = query.shape[0]
    scores = dot(query, key, 1, 1) * HD**-0.5
    allowed = lax.broadcasted_iota(jnp.int32, (seq, seq), 1) <= lax.broadcasted_iota(jnp.int32, (seq, seq), 0)
    scores = jnp.where(allowed, scores, -jnp.inf)
    raised = jnp.exp(scores - jnp.max(scores, axis=-1, keepdims=True))
    return raised / jnp.sum(raised, axis=-1, keepdims=True)


def expect(dst, sems, place, peer, left=False):
    copy = pltpu.make_async_remote_copy(
        src_ref=dst,
        dst_ref=dst,
        send_sem=sems.at[(0, *place)],
        recv_sem=sems.at[(1, *place)],
        device_id=peer,
        device_id_type=MESH,
    )
    if left:
        copy.wait_send()
    else:
        copy.wait_recv()


def stage_kernel(mode, owner, count, model, *refs):
    if mode == "forward":
        part, stat, raw_out, proj, stat_out, result, landed, stats, scatter, gather, via, small, fanned = refs
    elif mode == "both":
        part, stat, grads, result, coef_out, mixed_out = refs[:6]
        landed, stats, proj, scatter, gather, via, small, hops, lands, fanned = refs[6:]
    else:
        part, proj, stat, result, landed, probs_all, scatter, gather, via, hops, lands, fanned = refs
    me = lax.axis_index("dp")
    section = lax.axis_index("pipe")
    mine = section == owner
    partner = {"pipe": 1 - section}
    peers = others("dp")
    meet([{"dp": p} for p in peers] + [partner])
    groups = scatter.shape[1]
    seq = part.shape[1]
    cols = part.shape[2] // groups
    full = (GROUP + 2) * HD
    low = GROUP * HD
    last = groups - 1
    steps = list(range(1, count))
    last_part = pl.ds(last * cols, cols)
    last_out = pl.ds(last * low, low) if mode == "forward" else pl.ds(last * full, full)
    copies = []

    def scatter_direct(g):
        strip = pl.ds(g * cols, cols)
        for step, peer in enumerate(peers, 1):
            block = part.at[peer, :, strip]
            copies.append(push(block, landed.at[step, :, strip], scatter, (g, step), {"dp": peer}))

    def take_stats():
        squares = stat[me]
        for step, peer in enumerate(peers, 1):
            expect(stats.at[step], small, (0, step), {"dp": peer})
            squares = squares + stats[step]
        return squares

    def send_stats():
        for step, peer in enumerate(peers, 1):
            copies.append(push(stat.at[peer], stats.at[step], small, (0, step), {"dp": peer}))

    def arrived(g):
        strip = pl.ds(g * cols, cols)
        for step, peer in enumerate(peers, 1):
            if g == last and mode != "forward":
                expect(landed.at[step, :, strip], via, (2, step), partner)
            else:
                expect(landed.at[step, :, strip], scatter, (g, step), {"dp": peer})

    def total(at):
        sums = part[me, :, at].astype(F32)
        for step in steps:
            sums = sums + landed[step, :, at].astype(F32)
        return sums

    def project(g, recip):
        for i in range(GROUP + 2):
            at = pl.ds(g * full + i * HD, HD)
            raw = total(at)
            if mode == "forward":
                raw_out[:, at] = raw.astype(BF)
            proj[:, at] = (raw * recip).astype(BF)

    def work(g, recip, coef):
        base = g * full
        key, value = proj[:, pl.ds(base + low, HD)], proj[:, pl.ds(base + low + HD, HD)]
        grad_key = jnp.zeros((seq, HD), F32)
        grad_value = jnp.zeros((seq, HD), F32)
        for j in range(GROUP):
            at = pl.ds(base + j * HD, HD)
            mixed_at = pl.ds(g * low + j * HD, HD)
            query = proj[:, at]
            probs = probs_all[g * GROUP + j] if mode == "backward" else probs_of(query, key)
            probs_low = probs.astype(BF)
            if mode != "backward":
                mixed = dot(probs_low, value, 1, 0).astype(BF)
            if mode == "forward":
                result[me, :, mixed_at] = mixed
                continue
            if mode == "both":
                mixed_out[:, mixed_at] = mixed
                grad = grads[:, mixed_at]
            else:
                grad = total(mixed_at).astype(BF)
            grad_low = dot(grad, value, 1, 1)
            inner = jnp.sum(probs * grad_low, axis=-1, keepdims=True)
            grad_score = (probs * (grad_low - inner) * HD**-0.5).astype(BF)
            grad_query = dot(grad_score, key, 1, 0)
            grad_key = grad_key + dot(grad_score, query, 0, 0)
            grad_value = grad_value + dot(probs_low, grad, 0, 0)
            result[me, :, at] = (grad_query * recip).astype(BF)
            if mode == "both":
                coef = coef + jnp.sum(grad_query * query.astype(F32), axis=-1, keepdims=True)
        if mode == "forward":
            strip = pl.ds(g * low, low)
        else:
            strip = pl.ds(base, full)
            result[me, :, pl.ds(base + low, HD)] = (grad_key * recip).astype(BF)
            result[me, :, pl.ds(base + low + HD, HD)] = (grad_value * recip).astype(BF)
            if mode == "both":
                coef = coef + jnp.sum(grad_key * key.astype(F32), axis=-1, keepdims=True)
                coef = coef + jnp.sum(grad_value * value.astype(F32), axis=-1, keepdims=True)
        block = result.at[me, :, strip]
        if g == last:
            push(block, fanned.at[0], via, (3, 0), partner)
        else:
            for step, peer in enumerate(peers, 1):
                push(block, block, gather, (g, step), {"dp": peer})
        return coef

    def collect():
        for g in range(last):
            strip = pl.ds(g * low, low) if mode == "forward" else pl.ds(g * full, full)
            for step, peer in enumerate(peers, 1):
                source = lax.rem(me + count - step, count)
                expect(result.at[source, :, strip], gather, (g, step), {"dp": peer})
        for step in steps:
            source = lax.rem(me + count - step, count)
            expect(result.at[source, :, last_out], via, (5, step), partner)
        for g in range(last):
            strip = pl.ds(g * low, low) if mode == "forward" else pl.ds(g * full, full)
            for step, peer in enumerate(peers, 1):
                expect(result.at[me, :, strip], gather, (g, step), {"dp": peer}, True)
        expect(result.at[me, :, last_out], via, (3, 0), partner, True)

    def help_gather():
        sent = []
        expect(fanned.at[0], via, (3, 0), partner)
        for step, peer in enumerate(peers, 1):
            sent.append(push(fanned.at[0], fanned.at[step], via, (4, step), {"dp": peer}))
        for step, peer in enumerate(peers, 1):
            source = lax.rem(me + count - step, count)
            expect(fanned.at[step], via, (4, step), {"dp": peer})
            sent.append(push(fanned.at[step], result.at[source, :, last_out], via, (5, step), partner))
        for copy in sent:
            copy.wait_send()

    if mode == "forward":
        send_stats()
        for g in range(groups):
            scatter_direct(g)
        squares = take_stats()
        stat_out[...] = squares
        recip = lax.rsqrt(column(squares[0:1, :]) / model + EPSILON)
        for g in range(groups):
            arrived(g)
            project(g, recip)

            @pl.when(mine)
            def attention(g=g):
                work(g, recip, None)

        pl.when(mine)(collect)
        pl.when(section != owner)(help_gather)
        for copy in copies:
            copy.wait_send()
        return

    @pl.when(mine)
    def owning():
        if mode == "both":
            send_stats()
        for step, peer in enumerate(peers, 1):
            copies.append(push(part.at[peer, :, last_part], hops.at[step], via, (0, step), partner))
        for g in range(last):
            scatter_direct(g)
        if mode == "backward":
            squares = stat[...]
            for g in range(groups):
                key = proj[:, pl.ds(g * full + low, HD)]
                for j in range(GROUP):
                    probs_all[g * GROUP + j] = probs_of(proj[:, pl.ds(g * full + j * HD, HD)], key)
        else:
            squares = take_stats()
        recip = lax.rsqrt(column(squares[0:1, :]) / model + EPSILON)
        coef = jnp.zeros((seq, 1), F32)
        sent = []
        for g in range(groups):
            arrived(g)
            if mode == "both":
                project(g, recip)
            coef = work(g, recip, coef)
        if mode == "both":
            coef_out[me] = jnp.broadcast_to(as_row(coef * recip * recip / model), coef_out.shape[1:])
            for step, peer in enumerate(peers, 1):
                block = coef_out.at[me]
                sent.append(push(block, block, small, (1, step), {"dp": peer}))
            for step, peer in enumerate(peers, 1):
                source = lax.rem(me + count - step, count)
                expect(coef_out.at[source], small, (1, step), {"dp": peer})
        collect()
        for copy in copies + sent:
            copy.wait_send()

    @pl.when(section != owner)
    def helping():
        passed = []

        def onward(step):
            expect(hops.at[step], via, (0, step), partner)
            passed.append(push(hops.at[step], lands.at[step], via, (1, step), {"dp": peers[step - 1]}))

        def home(step):
            expect(lands.at[step], via, (1, step), {"dp": peers[step - 1]})
            passed.append(push(lands.at[step], landed.at[step, :, last_part], via, (2, step), partner))

        onward(1)
        for step in steps:
            if step + 1 < count:
                onward(step + 1)
            home(step)
        for copy in passed:
            copy.wait_send()
        help_gather()


def stage(mode, owner, arrays, groups, model, collective_id):
    part = arrays[0]
    count, seq, cols = part.shape
    full = groups * (GROUP + 2) * HD
    low = groups * GROUP * HD
    dma = pltpu.SemaphoreType.DMA
    sems = [dma((2, groups, count)), dma((2, groups, count)), dma((2, 6, count))]
    landed = pltpu.VMEM(part.shape, BF)
    hop = pltpu.VMEM((count, seq, cols // groups), BF)
    fanned = pltpu.VMEM((count, seq, (low if mode == "forward" else full) // groups), BF)
    stats = pltpu.VMEM((count, 8, seq), F32)
    if mode == "backward":
        outs = [((count, seq, full), BF)]
        scratch = [landed, pltpu.VMEM((groups * GROUP, seq, seq), F32), *sems, hop, hop, fanned]
    elif mode == "forward":
        outs = [((seq, full), BF), ((seq, full), BF), ((8, seq), F32), ((count, seq, low), BF)]
        scratch = [landed, stats, *sems, dma((2, 2, count)), fanned]
    else:
        outs = [((count, seq, full), BF), ((count, 8, seq), F32), ((seq, low), BF)]
        scratch = [landed, stats, pltpu.VMEM((seq, full), BF), *sems, dma((2, 2, count)), hop, hop, fanned]
    kernel = functools.partial(stage_kernel, mode, owner, count, model)
    return call(kernel, collective_id, arrays, outs, scratch)


def total_kernel(count, in_ref, out_ref, landed, sems):
    meet([{"tensor": p} for p in others("tensor")])
    copies = [
        push(in_ref, landed.at[step], sems, (step,), {"tensor": peer})
        for step, peer in enumerate(others("tensor"), 1)
    ]
    total = in_ref[...]
    for step, copy in enumerate(copies, 1):
        copy.wait_recv()
        total = total + landed[step]
    out_ref[...] = total
    for copy in copies:
        copy.wait_send()


def tensor_total(array, collective_id):
    count = lax.axis_size("tensor")
    scratch = [pltpu.VMEM((count, *array.shape), F32), pltpu.SemaphoreType.DMA((2, count))]
    return call(functools.partial(total_kernel, count), collective_id, [array], [(array.shape, F32)], scratch)[0]


def shards(tokens, norm_gains, qkv_weight, out_weight, cotangent):
    first = lax.axis_index("pipe") == 0
    count = lax.axis_size("dp")
    qkv, out = qkv_weight[0], out_weight[0]
    width, cols = qkv.shape
    head_cols = out.shape[1]
    seq, model = tokens.shape[1:]
    rows = count * seq
    groups = cols // ((GROUP + 2) * HD)
    gain = lax.dynamic_slice_in_dim(norm_gains[0], lax.axis_index("dp") * width, width, 0)[None]

    def project(block):
        scaled = block.astype(F32)
        squares = jnp.sum(scaled * scaled, axis=-1).reshape(count, 1, seq)
        squares = jnp.broadcast_to(squares, (count, 8, seq))
        return dot((scaled * gain).astype(BF), qkv, 1, 0).astype(BF), squares

    held = spread(tokens[0], cotangent[0], width, 0).reshape(rows, width)

    proj_part, squares = project(held)
    mixed_part = jnp.pad(dot(held, out, 1, 0).astype(BF), ((0, 0), (0, cols - head_cols)))
    part = jnp.where(first, proj_part, mixed_part).reshape(count, seq, cols)
    grads, proj, squares, mixed_start = stage("forward", 0, [part, squares], groups, model, 1)
    mixed_start = mixed_start.reshape(rows, head_cols)
    carried = relay(dot(mixed_start, out, 1, 1).astype(BF), held, 2)

    part, next_squares = project(carried)
    part = part.reshape(count, seq, cols)
    grad_proj_next, coef, mixed = stage("both", 1, [part, next_squares, grads], groups, model, 3)
    grad_proj_next = grad_proj_next.reshape(rows, cols)
    coef = coef[:, 0].reshape(rows, 1)
    back = dot(grad_proj_next, qkv, 1, 1) * gain - carried.astype(F32) * coef
    returned, mixed_next = relay(back.astype(BF), held, 4, mixed)

    part = dot(returned, out, 1, 0).astype(BF).reshape(count, seq, head_cols)
    (grad_proj,) = stage("backward", 0, [part, proj, squares], groups, model, 5)

    block_in = jnp.where(first, held, carried)
    grad_out = jnp.where(first, returned, held)
    mixed_all = jnp.where(first, mixed_start, mixed_next.reshape(rows, head_cols))
    grad_proj = jnp.where(first, grad_proj.reshape(rows, cols), grad_proj_next)
    out_grad = dot(grad_out, mixed_all, 0, 0)
    weight = dot(block_in, grad_proj, 0, 0)
    qkv_grad = weight * gain.reshape(width, 1)
    gain_part = jnp.sum(weight * qkv.astype(F32), axis=-1)
    gain_grad = tensor_total(gain_part.reshape(width // 128, 128), 6).reshape(1, width)
    return qkv_grad[None], out_grad[None], gain_grad


def solution(mesh):
    in_specs = (
        P("dp", None, None),
        P("pipe", None),
        P("pipe", "dp", "tensor"),
        P("pipe", "dp", "tensor"),
        P("dp", None, None),
    )
    out_specs = (P("pipe", "dp", "tensor"), P("pipe", "dp", "tensor"), P("pipe", "dp"))
    return jax.shard_map(shards, mesh=mesh, in_specs=in_specs, out_specs=out_specs, check_vma=False)
```

```python
import functools

import jax
import jax.numpy as jnp
from jax import lax
from jax.experimental import pallas as pl
from jax.experimental.pallas import tpu as pltpu
from jax.sharding import PartitionSpec as P

HD = 128
GROUP = 4
EPSILON = 1e-05
PIECES = 2
BF = jnp.bfloat16
F32 = jnp.float32
MESH = pl.DeviceIdType.MESH


def dot(a, b, ca, cb):
    return lax.dot_general(a, b, (((ca,), (cb,)), ((), ())), preferred_element_type=F32)


def meet(peers):
    barrier = pltpu.get_barrier_semaphore()
    for peer in peers:
        pl.semaphore_signal(barrier, inc=1, device_id=peer, device_id_type=MESH)
    pl.semaphore_wait(barrier, len(peers))


def others(axis):
    me, count = lax.axis_index(axis), lax.axis_size(axis)
    return [lax.rem(me + step, count) for step in range(1, count)]


def push(src, dst, sems, place, peer):
    copy = pltpu.make_async_remote_copy(
        src_ref=src,
        dst_ref=dst,
        send_sem=sems.at[(0, *place)],
        recv_sem=sems.at[(1, *place)],
        device_id=peer,
        device_id_type=MESH,
    )
    copy.start()
    return copy


def beside():
    tensor = lax.axis_index("tensor")
    core, chip = lax.rem(tensor, 2), tensor // 2
    return tensor, core, chip, chip * 2 + 1 - core, (1 - chip) * 2 + core


def call(kernel, collective_id, arrays, outs, scratch):
    vmem = pl.BlockSpec(memory_space=pltpu.VMEM)
    return pl.pallas_call(
        kernel,
        out_shape=[jax.ShapeDtypeStruct(shape, dtype) for shape, dtype in outs],
        in_specs=[vmem] * len(arrays),
        out_specs=[vmem] * len(outs),
        scratch_shapes=scratch,
        compiler_params=pltpu.CompilerParams(
            collective_id=collective_id, has_side_effects=True, vmem_limit_bytes=48 << 20
        ),
    )(*arrays)


def spread_kernel(count, tokens_ref, cotangent_ref, out_ref, picked, dp_sems, chip_sems, core_sems, far_sems):
    me = lax.axis_index("dp")
    tensor, core, chip, sibling, across = beside()
    peers = others("dp")
    meet([{"dp": p} for p in peers] + [{"tensor": sibling}, {"tensor": across}])
    rows, width = picked.shape[0], out_ref.shape[2]
    mine = pl.ds(pl.multiple_of(tensor * rows, rows), rows)
    far = pl.ds(pl.multiple_of(across * rows, rows), rows)
    first = lax.axis_index("pipe") == 0
    picked[...] = jnp.where(first, tokens_ref[mine, :], cotangent_ref[mine, :])
    copies, later = [], []
    for step, peer in enumerate(peers, 1):
        block = picked.at[:, pl.ds(pl.multiple_of(peer * width, width), width)]
        copies.append(push(block, out_ref.at[me, mine], dp_sems, (step,), {"dp": peer}))
    out_ref[me, mine, :] = picked[:, pl.ds(pl.multiple_of(me * width, width), width)]
    for step in range(count):
        source = lax.rem(me + count - step, count)
        if step:
            copies[step - 1].wait_recv()
        block = out_ref.at[source, mine]
        later.append(push(block, block, chip_sems, (step,), {"tensor": across}))
        copies.append(push(block, block, core_sems, (step,), {"tensor": sibling}))
    for step in range(count):
        source = lax.rem(me + count - step, count)
        later[step].wait_recv()
        block = out_ref.at[source, far]
        copies.append(push(block, block, far_sems, (step,), {"tensor": sibling}))
    for step, copy in enumerate(copies):
        if step >= count - 1:
            copy.wait_recv()
        copy.wait_send()
    for copy in later:
        copy.wait_send()


def spread(tokens, cotangent, width, collective_id):
    count = lax.axis_size("dp")
    seq, model = tokens.shape
    dma = pltpu.SemaphoreType.DMA((2, count))
    (out,) = call(
        functools.partial(spread_kernel, count),
        collective_id,
        [tokens, cotangent],
        [((count, seq, width), BF)],
        [pltpu.VMEM((seq // lax.axis_size("tensor"), model), BF), dma, dma, dma, dma],
    )
    return out


def relay_kernel(chunks, beside_z, *refs):
    if beside_z:
        part_ref, rest_ref, extra_ref, out_ref, gathered = refs[:5]
        near, half, landed, own, core_sems, sems, dp_sems = refs[5:]
    else:
        part_ref, rest_ref, out_ref, near, half, landed, own, core_sems, sems = refs
    tensor, core, chip, sibling, across = beside()
    section = {"pipe": 1 - lax.axis_index("pipe")}
    me = lax.axis_index("dp")
    peers = others("dp") if beside_z else []
    meet([{"dp": p} for p in peers] + [{"tensor": sibling}, {"tensor": across}, section])
    sibling_to, across_to = {"tensor": sibling}, {"tensor": across}
    rows = own.shape[0] // chunks
    cut = [pl.ds(k * rows, rows) for k in range(chunks)]
    held, firsts, seconds, across_x, fans, ends = [], [], [], [], [], []
    for k in range(chunks):
        give = (1 - chip) * 2 + 1 - core
        firsts.append(push(part_ref.at[give, cut[k]], near.at[0, cut[k]], core_sems, (0, k), sibling_to))
    for k in range(chunks):
        held.append(push(part_ref.at[sibling, cut[k]], near.at[1, cut[k]], core_sems, (1, k), sibling_to))
    for step, peer in enumerate(peers, 1):
        seconds.append(push(extra_ref, gathered.at[me], dp_sems, (step,), {"dp": peer}))
    if beside_z:
        gathered[me] = extra_ref[...]
    outs = []
    for k in range(chunks):
        firsts[k].wait_recv()
        half[cut[k], :] = (part_ref[across, cut[k], :].astype(F32) + near[0, cut[k], :].astype(F32)).astype(BF)
        outs.append(push(half.at[cut[k]], landed.at[cut[k]], sems, (0, k), across_to))
    for k in range(chunks):
        held[k].wait_recv()
        total = rest_ref[cut[k], :].astype(F32) + part_ref[tensor, cut[k], :].astype(F32)
        total = total + near[1, cut[k], :].astype(F32)
        outs[k].wait_recv()
        own[cut[k], :] = (total + landed[cut[k], :].astype(F32)).astype(BF)
        across_x.append(push(own.at[cut[k]], out_ref.at[tensor, cut[k]], sems, (1, k), section))
    for k in range(chunks):
        across_x[k].wait_recv()
        block = out_ref.at[tensor, cut[k]]
        fans.append(push(block, block, sems, (2, k), across_to))
        ends.append(push(block, block, core_sems, (2, k), sibling_to))
    for k in range(chunks):
        fans[k].wait_recv()
        block = out_ref.at[across, cut[k]]
        ends.append(push(block, block, core_sems, (3, k), sibling_to))
    for copy in ends + seconds:
        copy.wait_recv()
    for copy in firsts + held + outs + across_x + fans + ends + seconds:
        copy.wait_send()


def relay(parts, rest, collective_id, extra=None):
    count, dp = lax.axis_size("tensor"), lax.axis_size("dp")
    rows, width = parts.shape[0] // count, parts.shape[1]
    chunks = 4
    parts = parts.reshape(count, rows, width)
    own = lax.dynamic_index_in_dim(rest.reshape(count, rows, width), lax.axis_index("tensor"), 0, False)
    more = [] if extra is None else [extra]
    block = pltpu.VMEM((rows, width), BF)
    results = call(
        functools.partial(relay_kernel, chunks, bool(more)),
        collective_id,
        [parts, own] + more,
        [(parts.shape, BF)] + [((dp, *a.shape), a.dtype) for a in more],
        [
            pltpu.VMEM((2, rows, width), BF),
            block,
            block,
            block,
            pltpu.SemaphoreType.DMA((2, 4, chunks)),
            pltpu.SemaphoreType.DMA((2, 3, chunks)),
        ]
        + [pltpu.SemaphoreType.DMA((2, dp)) for a in more],
    )
    out = results[0].reshape(count * rows, width)
    return (out, results[1]) if more else out


def column(row):
    size = row.shape[1]
    same = lax.broadcasted_iota(jnp.int32, (size, size), 0) == lax.broadcasted_iota(jnp.int32, (size, size), 1)
    return jnp.sum(jnp.where(same, row, 0.0), axis=1, keepdims=True)


def as_row(col):
    size = col.shape[0]
    same = lax.broadcasted_iota(jnp.int32, (size, size), 0) == lax.broadcasted_iota(jnp.int32, (size, size), 1)
    return jnp.sum(jnp.where(same, col, 0.0), axis=0, keepdims=True)


def head(index):
    return pl.ds(index * HD, HD)


def probs_of(query, key):
    seq = query.shape[0]
    scores = dot(query, key, 1, 1) * HD**-0.5
    allowed = lax.broadcasted_iota(jnp.int32, (seq, seq), 1) <= lax.broadcasted_iota(jnp.int32, (seq, seq), 0)
    scores = jnp.where(allowed, scores, -jnp.inf)
    raised = jnp.exp(scores - jnp.max(scores, axis=-1, keepdims=True))
    return raised / jnp.sum(raised, axis=-1, keepdims=True)


def expect(dst, sems, place, peer, left=False):
    copy = pltpu.make_async_remote_copy(
        src_ref=dst,
        dst_ref=dst,
        send_sem=sems.at[(0, *place)],
        recv_sem=sems.at[(1, *place)],
        device_id=peer,
        device_id_type=MESH,
    )
    if left:
        copy.wait_send()
    else:
        copy.wait_recv()


def stage_kernel(mode, owner, count, model, *refs):
    if mode == "forward":
        part, stat, raw_out, proj, stat_out, result, landed, stats, scatter, gather, via, small = refs
    elif mode == "both":
        part, stat, grads, result, coef_out, mixed_out = refs[:6]
        landed, stats, proj, scatter, gather, via, small, hops, lands, fanned = refs[6:]
    else:
        part, proj, stat, result, landed, probs_all, scatter, gather, via, hops, lands, fanned = refs
    me = lax.axis_index("dp")
    section = lax.axis_index("pipe")
    mine = section == owner
    partner = {"pipe": 1 - section}
    peers = others("dp")
    meet([{"dp": p} for p in peers] + [partner])
    groups = scatter.shape[1]
    seq = part.shape[1]
    cols = part.shape[2] // groups
    full = (GROUP + 2) * HD
    low = GROUP * HD
    last = groups - 1
    steps = list(range(1, count))
    direct = groups if mode == "forward" else last
    pieces = [(i, pl.ds(i * (seq // PIECES), seq // PIECES)) for i in range(PIECES)]
    last_part = pl.ds(last * cols, cols)
    last_out = pl.ds(last * low, low) if mode == "forward" else pl.ds(last * full, full)
    copies = []

    def scatter_direct(g):
        strip = pl.ds(g * cols, cols)
        for step, peer in enumerate(peers, 1):
            block = part.at[peer, :, strip]
            copies.append(push(block, landed.at[step, :, strip], scatter, (g, step), {"dp": peer}))

    def take_stats():
        squares = stat[me]
        for step, peer in enumerate(peers, 1):
            expect(stats.at[step], small, (0, step), {"dp": peer})
            squares = squares + stats[step]
        return squares

    def send_stats():
        for step, peer in enumerate(peers, 1):
            copies.append(push(stat.at[peer], stats.at[step], small, (0, step), {"dp": peer}))

    def arrived(g):
        strip = pl.ds(g * cols, cols)
        for step, peer in enumerate(peers, 1):
            if g == last and mode != "forward":
                for i, cut in pieces:
                    expect(landed.at[step, cut, strip], via, (2, step, i), partner)
            else:
                expect(landed.at[step, :, strip], scatter, (g, step), {"dp": peer})

    def total(at):
        sums = part[me, :, at].astype(F32)
        for step in steps:
            sums = sums + landed[step, :, at].astype(F32)
        return sums

    def project(g, recip):
        for i in range(GROUP + 2):
            at = pl.ds(g * full + i * HD, HD)
            raw = total(at)
            if mode == "forward":
                raw_out[:, at] = raw.astype(BF)
            proj[:, at] = (raw * recip).astype(BF)

    def work(g, recip, coef):
        base = g * full
        key, value = proj[:, pl.ds(base + low, HD)], proj[:, pl.ds(base + low + HD, HD)]
        grad_key = jnp.zeros((seq, HD), F32)
        grad_value = jnp.zeros((seq, HD), F32)
        for j in range(GROUP):
            at = pl.ds(base + j * HD, HD)
            mixed_at = pl.ds(g * low + j * HD, HD)
            query = proj[:, at]
            probs = probs_all[g * GROUP + j] if mode == "backward" else probs_of(query, key)
            probs_low = probs.astype(BF)
            if mode != "backward":
                mixed = dot(probs_low, value, 1, 0).astype(BF)
            if mode == "forward":
                result[me, :, mixed_at] = mixed
                continue
            if mode == "both":
                mixed_out[:, mixed_at] = mixed
                grad = grads[:, mixed_at]
            else:
                grad = total(mixed_at).astype(BF)
            grad_low = dot(grad, value, 1, 1)
            inner = jnp.sum(probs * grad_low, axis=-1, keepdims=True)
            grad_score = (probs * (grad_low - inner) * HD**-0.5).astype(BF)
            grad_query = dot(grad_score, key, 1, 0)
            grad_key = grad_key + dot(grad_score, query, 0, 0)
            grad_value = grad_value + dot(probs_low, grad, 0, 0)
            result[me, :, at] = (grad_query * recip).astype(BF)
            if mode == "both":
                coef = coef + jnp.sum(grad_query * query.astype(F32), axis=-1, keepdims=True)
        if mode == "forward":
            strip = pl.ds(g * low, low)
        else:
            strip = pl.ds(base, full)
            result[me, :, pl.ds(base + low, HD)] = (grad_key * recip).astype(BF)
            result[me, :, pl.ds(base + low + HD, HD)] = (grad_value * recip).astype(BF)
            if mode == "both":
                coef = coef + jnp.sum(grad_key * key.astype(F32), axis=-1, keepdims=True)
                coef = coef + jnp.sum(grad_value * value.astype(F32), axis=-1, keepdims=True)
        block = result.at[me, :, strip]
        if g >= direct:
            for i, cut in pieces:
                push(result.at[me, cut, strip], fanned.at[0, cut], via, (3, 0, i), partner)
        else:
            for step, peer in enumerate(peers, 1):
                push(block, block, gather, (g, step), {"dp": peer})
        return coef

    def collect():
        for g in range(direct):
            strip = pl.ds(g * low, low) if mode == "forward" else pl.ds(g * full, full)
            for step, peer in enumerate(peers, 1):
                source = lax.rem(me + count - step, count)
                expect(result.at[source, :, strip], gather, (g, step), {"dp": peer})
        for step in steps if direct < groups else []:
            source = lax.rem(me + count - step, count)
            for i, cut in pieces:
                expect(result.at[source, cut, last_out], via, (5, step, i), partner)
        for g in range(direct):
            strip = pl.ds(g * low, low) if mode == "forward" else pl.ds(g * full, full)
            for step, peer in enumerate(peers, 1):
                expect(result.at[me, :, strip], gather, (g, step), {"dp": peer}, True)
        for i, cut in pieces if direct < groups else []:
            expect(result.at[me, cut, last_out], via, (3, 0, i), partner, True)

    def help_gather():
        sent = []
        for i, cut in pieces:
            expect(fanned.at[0, cut], via, (3, 0, i), partner)
            for step, peer in enumerate(peers, 1):
                sent.append(push(fanned.at[0, cut], fanned.at[step, cut], via, (4, step, i), {"dp": peer}))
        for i, cut in pieces:
            for step, peer in enumerate(peers, 1):
                source = lax.rem(me + count - step, count)
                expect(fanned.at[step, cut], via, (4, step, i), {"dp": peer})
                home = result.at[source, cut, last_out]
                sent.append(push(fanned.at[step, cut], home, via, (5, step, i), partner))
        for copy in sent:
            copy.wait_send()

    if mode == "forward":
        send_stats()
        for g in range(groups):
            scatter_direct(g)
        squares = take_stats()
        stat_out[...] = squares
        recip = lax.rsqrt(column(squares[0:1, :]) / model + EPSILON)
        for g in range(groups):
            arrived(g)
            project(g, recip)

            @pl.when(mine)
            def attention(g=g):
                work(g, recip, None)

        pl.when(mine)(collect)
        for copy in copies:
            copy.wait_send()
        return

    @pl.when(mine)
    def owning():
        if mode == "both":
            send_stats()
        for step, peer in enumerate(peers, 1):
            for i, cut in pieces:
                block = part.at[peer, cut, last_part]
                copies.append(push(block, hops.at[step, cut], via, (0, step, i), partner))
        for g in range(last):
            scatter_direct(g)
        if mode == "backward":
            squares = stat[...]
            for g in range(groups):
                key = proj[:, pl.ds(g * full + low, HD)]
                for j in range(GROUP):
                    probs_all[g * GROUP + j] = probs_of(proj[:, pl.ds(g * full + j * HD, HD)], key)
        else:
            squares = take_stats()
        recip = lax.rsqrt(column(squares[0:1, :]) / model + EPSILON)
        coef = jnp.zeros((seq, 1), F32)
        sent = []
        for g in range(groups):
            arrived(g)
            if mode == "both":
                project(g, recip)
            coef = work(g, recip, coef)
        if mode == "both":
            coef_out[me] = jnp.broadcast_to(as_row(coef * recip * recip / model), coef_out.shape[1:])
            for step, peer in enumerate(peers, 1):
                block = coef_out.at[me]
                sent.append(push(block, block, small, (1, step), {"dp": peer}))
            for step, peer in enumerate(peers, 1):
                source = lax.rem(me + count - step, count)
                expect(coef_out.at[source], small, (1, step), {"dp": peer})
        collect()
        for copy in copies + sent:
            copy.wait_send()

    @pl.when(section != owner)
    def helping():
        passed = []

        def onward(step, i, cut):
            expect(hops.at[step, cut], via, (0, step, i), partner)
            peer = {"dp": peers[step - 1]}
            passed.append(push(hops.at[step, cut], lands.at[step, cut], via, (1, step, i), peer))

        def home(step, i, cut):
            expect(lands.at[step, cut], via, (1, step, i), {"dp": peers[step - 1]})
            block = landed.at[step, cut, last_part]
            passed.append(push(lands.at[step, cut], block, via, (2, step, i), partner))

        order = [(step, i, cut) for step in steps for i, cut in pieces]
        ahead = min(2, len(order))
        for item in order[:ahead]:
            onward(*item)
        for index, item in enumerate(order):
            if index + ahead < len(order):
                onward(*order[index + ahead])
            home(*item)
        for copy in passed:
            copy.wait_send()
        help_gather()


def stage(mode, owner, arrays, groups, model, collective_id):
    part = arrays[0]
    count, seq, cols = part.shape
    full = groups * (GROUP + 2) * HD
    low = groups * GROUP * HD
    dma = pltpu.SemaphoreType.DMA
    sems = [dma((2, groups, count)), dma((2, groups, count)), dma((2, 6, count, PIECES))]
    landed = pltpu.VMEM(part.shape, BF)
    hop = pltpu.VMEM((count, seq, cols // groups), BF)
    fanned = pltpu.VMEM((count, seq, (low if mode == "forward" else full) // groups), BF)
    stats = pltpu.VMEM((count, 8, seq), F32)
    if mode == "backward":
        outs = [((count, seq, full), BF)]
        scratch = [landed, pltpu.VMEM((groups * GROUP, seq, seq), F32), *sems, hop, hop, fanned]
    elif mode == "forward":
        outs = [((seq, full), BF), ((seq, full), BF), ((8, seq), F32), ((count, seq, low), BF)]
        scratch = [landed, stats, *sems, dma((2, 2, count))]
    else:
        outs = [((count, seq, full), BF), ((count, 8, seq), F32), ((seq, low), BF)]
        scratch = [landed, stats, pltpu.VMEM((seq, full), BF), *sems, dma((2, 2, count)), hop, hop, fanned]
    kernel = functools.partial(stage_kernel, mode, owner, count, model)
    return call(kernel, collective_id, arrays, outs, scratch)


def total_kernel(count, in_ref, out_ref, landed, sems):
    meet([{"tensor": p} for p in others("tensor")])
    copies = [
        push(in_ref, landed.at[step], sems, (step,), {"tensor": peer})
        for step, peer in enumerate(others("tensor"), 1)
    ]
    total = in_ref[...]
    for step, copy in enumerate(copies, 1):
        copy.wait_recv()
        total = total + landed[step]
    out_ref[...] = total
    for copy in copies:
        copy.wait_send()


def tensor_total(array, collective_id):
    count = lax.axis_size("tensor")
    scratch = [pltpu.VMEM((count, *array.shape), F32), pltpu.SemaphoreType.DMA((2, count))]
    return call(functools.partial(total_kernel, count), collective_id, [array], [(array.shape, F32)], scratch)[0]


def shards(tokens, norm_gains, qkv_weight, out_weight, cotangent):
    first = lax.axis_index("pipe") == 0
    count = lax.axis_size("dp")
    qkv, out = qkv_weight[0], out_weight[0]
    width, cols = qkv.shape
    head_cols = out.shape[1]
    seq, model = tokens.shape[1:]
    rows = count * seq
    groups = cols // ((GROUP + 2) * HD)
    gain = lax.dynamic_slice_in_dim(norm_gains[0], lax.axis_index("dp") * width, width, 0)[None]

    def project(block):
        scaled = block.astype(F32)
        squares = jnp.sum(scaled * scaled, axis=-1).reshape(count, 1, seq)
        squares = jnp.broadcast_to(squares, (count, 8, seq))
        return dot((scaled * gain).astype(BF), qkv, 1, 0).astype(BF), squares

    held = spread(tokens[0], cotangent[0], width, 0).reshape(rows, width)

    proj_part, squares = project(held)
    mixed_part = jnp.pad(dot(held, out, 1, 0).astype(BF), ((0, 0), (0, cols - head_cols)))
    part = jnp.where(first, proj_part, mixed_part).reshape(count, seq, cols)
    grads, proj, squares, mixed_start = stage("forward", 0, [part, squares], groups, model, 1)
    mixed_start = mixed_start.reshape(rows, head_cols)
    carried = relay(dot(mixed_start, out, 1, 1).astype(BF), held, 2)

    part, next_squares = project(carried)
    part = part.reshape(count, seq, cols)
    grad_proj_next, coef, mixed = stage("both", 1, [part, next_squares, grads], groups, model, 3)
    grad_proj_next = grad_proj_next.reshape(rows, cols)
    coef = coef[:, 0].reshape(rows, 1)
    back = dot(grad_proj_next, qkv, 1, 1) * gain - carried.astype(F32) * coef
    returned, mixed_next = relay(back.astype(BF), held, 4, mixed)

    part = dot(returned, out, 1, 0).astype(BF).reshape(count, seq, head_cols)
    (grad_proj,) = stage("backward", 0, [part, proj, squares], groups, model, 5)

    block_in = jnp.where(first, held, carried)
    grad_out = jnp.where(first, returned, held)
    mixed_all = jnp.where(first, mixed_start, mixed_next.reshape(rows, head_cols))
    grad_proj = jnp.where(first, grad_proj.reshape(rows, cols), grad_proj_next)
    out_grad = dot(grad_out, mixed_all, 0, 0)
    weight = dot(block_in, grad_proj, 0, 0)
    qkv_grad = weight * gain.reshape(width, 1)
    gain_part = jnp.sum(weight * qkv.astype(F32), axis=-1)
    gain_grad = tensor_total(gain_part.reshape(width // 128, 128), 6).reshape(1, width)
    return qkv_grad[None], out_grad[None], gain_grad


def solution(mesh):
    in_specs = (
        P("dp", None, None),
        P("pipe", None),
        P("pipe", "dp", "tensor"),
        P("pipe", "dp", "tensor"),
        P("dp", None, None),
    )
    out_specs = (P("pipe", "dp", "tensor"), P("pipe", "dp", "tensor"), P("pipe", "dp"))
    return jax.shard_map(shards, mesh=mesh, in_specs=in_specs, out_specs=out_specs, check_vma=False)
```
